512 devices in a mesh: dp: 8 (over y, core), expert: 64 (over z, x).
Axes of the slice: x: 4, y: 4, z: 16, core: 2. Of those that a mesh axis runs over, the one named last changes fastest.
Arguments:
- activations: bfloat16 [32768, 2048], P(('dp', 'expert')), may hold values from -6 to 6
- curvature: bfloat16 [32768, 2048], P(('dp', 'expert')), may hold values from 0.099609375 to 10
- routes: int32 [32768, 8], P(('dp', 'expert')), may hold values from 0 to 63, all different within a row; in each aligned block of 64 rows (0 to 63, 64 to 127, ...) at most 9 rows name the same one
- route_gates: float32 [32768, 8], P(('dp', 'expert')), may hold values from 0.05 to 0.4
- w_gate: bfloat16 [64, 2048, 768], P('expert', 'dp'), may hold values from -0.125 to 0.125
- w_up: bfloat16 [64, 2048, 768], P('expert', 'dp'), may hold values from -0.125 to 0.125
- v_down: bfloat16 [64, 2048, 768], P('expert', 'dp'), may hold values from -0.21875 to 0.21875
Outputs:
- tangent_sum: float32 [32768, 2048], P(('dp', 'expert'))
- product_down: float32 [64, 2048, 768], P('expert', 'dp')
The draws below stay inside these ranges and needn't reach their ends.
Inputs may be any that keep to these rules, and one draw needn't show every extreme that they name: `routes`: each token names 8 different experts. In each aligned block of 64 tokens (the tokens of one device) no expert is named by more than 9 tokens, a bound that some block reaches.
All inputs are finite; a program needn't handle non-finite values.
Results may differ from the reference program's by a relative error of at most 0.017.
Values may be sent and summed in bfloat16 or wider, within the bound.
A program may use at most 64 MiB of HBM per device.

```python
import math
import jax
import jax.numpy as jnp
import numpy as np
from jax import lax

D = 2048
FF = 768
TOP = 8
TOK_DEV = 64
EXPERTS = 64
C = 9
TOKENS = 32768
N_DP = 8
DEVICES = 512


def steps_of(key, extent, pieces, least, largest):
    def one(axis_at, shards_of):
        draws = jax.random.uniform(jax.random.fold_in(jax.random.fold_in(key, 6), axis_at), (shards_of,), jnp.float32, least / len(pieces), largest / len(pieces))
        return jnp.repeat(jnp.exp(draws), extent[axis_at] // shards_of).reshape((-1,) + (1,) * (len(extent) - axis_at - 1))

    loudness = one(*pieces[0])
    for cut in pieces[1:]:
        loudness = loudness * one(*cut)
    return loudness


def routed_block(key, own, number, rows, amount, top, reach, slope):
    order = jax.random.permutation(key, amount)
    crowded, common = load_shares(amount, rows * top, reach, slope, True), load_shares(amount, rows * top, reach, slope, False)
    places = jnp.arange(amount)

    def named(tallies, offset_by):
        used = int((tallies > 0).sum())
        fixed = max(1, used // 4)
        shifted = fixed + (places - fixed + offset_by * (used - fixed)) % max(1, amount - fixed)
        return jnp.zeros((amount,), jnp.int32).at[order[jnp.where(places < fixed, places, shifted)]].set(jnp.asarray(tallies, jnp.int32))

    tallies = jnp.where(number % 4 == 0, named(crowded, number // 4), named(common, number - number // 4 - 1))
    mixed = jax.random.permutation(jax.random.fold_in(own, 3), amount)
    giver, taker = mixed[0:amount // 2 * 2:2], mixed[1:amount // 2 * 2:2]
    slack = jnp.minimum(tallies[giver] - 1, reach - tallies[taker]) // 2
    slack = jnp.where((giver == order[0]) | (taker == order[0]) | (tallies[taker] == 0), 0, jnp.maximum(slack, 0))
    shifted = jax.random.randint(jax.random.fold_in(own, 4), (amount // 2,), 0, 1 << 20) % (slack + 1)
    tallies = tallies.at[giver].add(-shifted).at[taker].add(shifted)
    members = jnp.searchsorted(jnp.cumsum(tallies), jnp.arange(rows * top), side="right").astype(jnp.int32)
    grid = members.reshape(top, rows).T
    grid = grid[jax.random.permutation(jax.random.fold_in(own, 1), rows)]
    offset_by = jax.random.randint(jax.random.fold_in(own, 2), (rows, 1), 0, top)
    return jnp.take_along_axis(grid, (jnp.arange(top)[None, :] + offset_by) % top, axis=1)


def load_shares(amount, total, limit, slope, full):
    weights = [(1 << 20) // math.isqrt(rank ** slope) + 1 for rank in range(1, amount + 1)]
    largest = limit if full else min(limit, max(-(-total // amount), total * weights[0] // sum(weights)))
    least = 1 if total - largest >= amount - 1 else 0
    holding, spare = [largest] + [least] * (amount - 1), total - largest - least * (amount - 1)
    while spare > 0:
        free = [i for i in range(1, amount) if holding[i] < largest] or [i for i in range(1, amount) if holding[i] < limit]
        pool, left = sum([weights[i] for i in free]), spare
        for i in free:
            more = min(limit - holding[i], max(1, left * weights[i] // pool), spare)
            holding[i] = holding[i] + more
            spare = spare - more
    return np.array(holding)


def gaussian(key, shape, scale, bound, pieces=(), held_as=jnp.bfloat16):
    values = scale * jax.random.normal(key, shape, jnp.float32)
    if pieces:
        values = values * steps_of(key, shape, pieces, -0.22, 0.18)
    return jnp.clip(values, -bound, bound).astype(held_as)


def setup_inputs(seed: int = 0) -> dict:
    key_of = jax.random.split(jax.random.key(seed), 8)
    activations = gaussian(key_of[0], (TOKENS, D), 1.0, 6.0, ((0, 512),))
    curvature = jnp.clip(jnp.exp(math.log(10.0) - 4.609084 * jax.random.uniform(key_of[1], (TOKENS, D), jnp.float32) ** steps_of(key_of[1], (TOKENS, D), ((0, 512),), -0.2, 0.2)), 0.099609375, 10.0).astype(jnp.bfloat16)
    routes_keys = jax.random.split(jax.random.fold_in(key_of[2], 1), TOKENS // TOK_DEV)
    routes_turns = jax.random.permutation(jax.random.fold_in(key_of[2], 3), TOKENS // TOK_DEV)
    routes = jax.vmap(lambda own, number: routed_block(jax.random.fold_in(key_of[2], 2), own, number, TOK_DEV, EXPERTS, TOP, C, 2))(routes_keys, routes_turns).reshape((TOKENS, TOP))
    route_gates = jnp.clip(0.05 + 0.35 * jax.random.uniform(key_of[3], (TOKENS, TOP), jnp.float32) ** steps_of(key_of[3], (TOKENS, TOP), ((0, 512),), -0.2, 0.2), 0.05, 0.4)
    w_gate = gaussian(key_of[4], (EXPERTS, D, FF), D ** -0.5, 0.125, ((0, 64), (1, 8)))
    w_up = gaussian(key_of[5], (EXPERTS, D, FF), D ** -0.5, 0.125, ((0, 64), (1, 8)))
    v_down = gaussian(key_of[6], (EXPERTS, D, FF), FF ** -0.5, 0.21875, ((0, 64), (1, 8)))
    return dict(activations=activations, curvature=curvature, routes=routes, route_gates=route_gates, w_gate=w_gate, w_up=w_up, v_down=v_down)


def reference(activations, curvature, routes, route_gates, w_gate, w_up, v_down):
    grouped = routes.reshape(DEVICES, TOK_DEV * TOP)
    chosen = (grouped[:, :, None] == jnp.arange(EXPERTS, dtype=jnp.int32)).astype(jnp.int32)
    earlier = jnp.cumsum(chosen, axis=1) - chosen
    slots = jnp.sum(chosen * earlier, axis=2).astype(jnp.int32)
    source = jnp.arange(DEVICES, dtype=jnp.int32)[:, None]
    where = (grouped * (DEVICES * C) + source * C + slots).reshape(-1)
    token_ids = jnp.broadcast_to(jnp.arange(TOKENS, dtype=jnp.int32)[:, None], (TOKENS, TOP)).reshape(-1)
    table = jnp.full((EXPERTS * DEVICES * C,), TOKENS, jnp.int32).at[where].set(token_ids).reshape(EXPERTS, DEVICES * C)
    weight_table = jnp.zeros((EXPERTS * DEVICES * C,), jnp.float32).at[where].set(route_gates.reshape(-1).astype(jnp.float32)).reshape(EXPERTS, DEVICES * C)
    padded = jnp.concatenate([activations, jnp.zeros((1, D), activations.dtype)], axis=0)

    def forward(carry, item):
        ids, weights, gate_w, up_w, dir_w = item
        rows = padded[ids]
        gate = jnp.dot(rows, gate_w, preferred_element_type=jnp.float32)
        up = jnp.dot(rows, up_w, preferred_element_type=jnp.float32)
        hidden = (jax.nn.silu(gate) * up).astype(jnp.bfloat16)
        back = jnp.dot(hidden, dir_w.T, preferred_element_type=jnp.float32).astype(jnp.bfloat16)
        carry = carry.at[ids].add(weights[:, None] * back.astype(jnp.float32))
        return carry, hidden

    total, hiddens = lax.scan(forward, jnp.zeros((TOKENS + 1, D), jnp.float32), (table, weight_table, w_gate, w_up, v_down))
    tangent = total[:TOKENS]
    scaled = jnp.concatenate([curvature.astype(jnp.float32) * tangent, jnp.zeros((1, D), jnp.float32)], axis=0)

    def block(item):
        ids, weights, hidden = item
        sent = (weights[:, None] * scaled[ids]).astype(jnp.bfloat16)
        parts = jnp.einsum('nrd,nrf->ndf', sent.reshape(N_DP, -1, D).astype(jnp.float32), hidden.reshape(N_DP, -1, FF).astype(jnp.float32))
        return jnp.sum(parts.astype(jnp.bfloat16).astype(jnp.float32), axis=0)

    product = lax.map(block, (table, weight_table, hiddens))
    return tangent, product
```

```python
import jax
import jax.numpy as jnp
from jax import lax
from jax.sharding import PartitionSpec as P

X = 4


def per_device(activations, curvature, routes, route_gates, w_gate, w_up, v_down):
    tokens, width = activations.shape
    experts = lax.axis_size("expert")
    top = routes.shape[1]
    capacity = max(2, 9 * top * tokens // (8 * experts))
    zs = experts // X
    columns = [[z * X + x for z in range(zs)] for x in range(X)]
    lines = [[z * X + x for x in range(X)] for z in range(zs)]
    my_z = lax.axis_index("expert") // X

    def gather_z(a):
        return lax.all_gather(a, "expert", axis=0, axis_index_groups=columns)

    def swap_x(rows):
        return lax.all_to_all(
            rows, "expert", split_axis=0, concat_axis=0, axis_index_groups=lines, tiled=True
        )

    full_gate = lax.all_gather(w_gate[0], "dp", axis=0, tiled=True)
    full_up = lax.all_gather(w_up[0], "dp", axis=0, tiled=True)
    full_down = lax.all_gather(v_down[0], "dp", axis=0, tiled=True)

    all_routes = gather_z(routes)
    all_gates = gather_z(route_gates)
    mine = my_z * X + jnp.arange(X, dtype=jnp.int32)
    match = all_routes[:, :, :, None] == mine
    chosen = jnp.any(match, axis=2)
    weight = jnp.sum(jnp.where(match, all_gates[:, :, :, None], 0.0), axis=2)
    count = chosen.astype(jnp.int32)
    slot = jnp.cumsum(count, axis=1) - count
    place = chosen[..., None] & (slot[..., None] == jnp.arange(capacity, dtype=jnp.int32))
    place = place.astype(jnp.float32)
    gated = place * weight[..., None]

    tokens_z = gather_z(activations)
    outgoing = jnp.einsum(
        "stxc,std->xscd", place.astype(jnp.bfloat16), tokens_z, preferred_element_type=jnp.float32
    ).astype(jnp.bfloat16)
    arrived = swap_x(outgoing).reshape(-1, width)
    gate = jnp.dot(arrived, full_gate, preferred_element_type=jnp.float32)
    up = jnp.dot(arrived, full_up, preferred_element_type=jnp.float32)
    hidden = (jax.nn.silu(gate) * up).astype(jnp.bfloat16)
    back = lax.dot_general(
        hidden, full_down, (((1,), (1,)), ((), ())), preferred_element_type=jnp.float32
    ).astype(jnp.bfloat16)
    returned = swap_x(back.reshape(X, zs, capacity, width))
    gated16 = gated.astype(jnp.bfloat16)
    partial = jnp.einsum(
        "stxc,xscd->std", gated16, returned, preferred_element_type=jnp.float32
    ).astype(jnp.bfloat16)
    tangent = lax.psum_scatter(
        partial, "expert", scatter_dimension=0, axis_index_groups=columns, tiled=False
    ).astype(jnp.float32)
    scaled = (curvature.astype(jnp.float32) * tangent).astype(jnp.bfloat16)
    scaled_z = gather_z(scaled)
    sending = jnp.einsum(
        "stxc,std->xscd", gated16, scaled_z, preferred_element_type=jnp.float32
    ).astype(jnp.bfloat16)
    received = swap_x(sending).reshape(-1, width)
    product = lax.psum_scatter(
        lax.dot_general(
            received, hidden, (((0,), (0,)), ((), ())), preferred_element_type=jnp.float32
        ).astype(jnp.bfloat16),
        "dp",
        scatter_dimension=0,
        tiled=True,
    ).astype(jnp.float32)
    return (tangent, product[None])


def solution(mesh):
    return jax.shard_map(
        per_device,
        mesh=mesh,
        in_specs=(
            P(("dp", "expert"), None),
            P(("dp", "expert"), None),
            P(("dp", "expert"), None),
            P(("dp", "expert"), None),
            P("expert", "dp", None),
            P("expert", "dp", None),
            P("expert", "dp", None),
        ),
        out_specs=(P(("dp", "expert"), None), P("expert", "dp", None)),
        check_vma=False,
    )
```

```python
import functools

import jax
import jax.numpy as jnp
from jax import lax
from jax.experimental import pallas as pl
from jax.experimental.pallas import tpu as pltpu
from jax.sharding import PartitionSpec as P

X = 4
Y = 4
HALF = 8
TOK = 64
CAP = 9
CHUNKS = 4
PAIR = 2 * TOK
GROUPS = ((1, 2, 3), (4, 5, 6), (7, 0))
ROWS = tuple(-(-len(g) * 2 * CAP // 16) * 16 for g in GROUPS)
STARTS = tuple(X * sum(ROWS[:g]) for g in range(len(GROUPS)))
TOTAL = X * sum(ROWS)
LAG = 1
MESH = pl.DeviceIdType.MESH
F32 = jnp.float32
BF16 = jnp.bfloat16


def dot(a, b, dims=((1,), (0,))):
    return lax.dot_general(a, b, (dims, ((), ())), preferred_element_type=F32)


def kernel(
    tok_ref, curv_ref, tab_ref, wg_ref, wu_ref, wd_ref, tan_ref, out_ref,
    wf, zb1, tb, qs, ws, pm0, pm1, pm2, gm0, gm1, gm2, gt0, gt1, gt2,
    st1, arr, hid, st2, br, rs_s, rs_r, sc, zb3, st3, rr, own, ps, pr, ys, yr,
    w_loc, w_ss, w_rs, f_ss, f_rs, z1_s, z1_r, t_s, t_r, x1_s, x1_r, x2_s, x2_r,
    rs_ss, rs_rs, z3_s, z3_r, x3_s, x3_r, p_s, p_r, y_s, y_r,
):
    pm, gm, gt = (pm0, pm1, pm2), (gm0, gm1, gm2), (gt0, gt1, gt2)
    dp = lax.axis_index("dp")
    e = lax.axis_index("expert")
    zi, xi = e // X, lax.rem(e, X)
    yi, ci = dp // 2, lax.rem(dp, 2)
    width = tok_ref.shape[1]
    cw = width // CHUNKS
    drows = wg_ref.shape[0]
    experts = 4 * HALF * 2

    def at_z(step):
        return (dp, lax.rem(e + step * X + experts, experts))

    def at_x(step):
        return (dp, zi * X + lax.rem(xi + step + X, X))

    def at_y(step):
        return (lax.rem(yi + step + Y, Y) * 2 + ci, e)

    sibling = (yi * 2 + (1 - ci), e)
    sends = []

    def remote(src, dst, ss, rs, dev):
        return pltpu.make_async_remote_copy(
            src_ref=src, dst_ref=dst, send_sem=ss, recv_sem=rs, device_id=dev, device_id_type=MESH
        )

    def go(copy):
        copy.start()
        sends.append(copy)

    barrier = pltpu.get_barrier_semaphore()
    partners = [at_z(1), at_z(-1), at_x(1), at_x(2), at_x(3), at_y(1), at_y(2), at_y(3), sibling]
    for dev in partners:
        pl.semaphore_signal(barrier, inc=1, device_id=dev, device_id_type=MESH)
    pl.semaphore_wait(barrier, len(partners))

    def z1_copy(d, k, j):
        src = tok_ref.at[:, j * cw : (j + 1) * cw] if k == 0 else zb1.at[d, k - 1, j]
        return remote(src, zb1.at[d, k, j], z1_s.at[d, k, j], z1_r.at[d, k, j], at_z(1 - 2 * d))

    def t_copy(d, k):
        src = tab_ref if k == 0 else tb.at[d, k - 1]
        return remote(src, tb.at[d, k], t_s.at[d, k], t_r.at[d, k], at_z(1 - 2 * d))

    def z3_copy(d, k, i):
        src = sc.at[i] if k == 0 else zb3.at[d, k - 1, i]
        return remote(src, zb3.at[d, k, i], z3_s.at[d, k, i], z3_r.at[d, k, i], at_z(1 - 2 * d))

    def rs_copy(d, s, i):
        return remote(
            rs_s.at[d, s, i], rs_r.at[d, s, i], rs_ss.at[d, s, i], rs_rs.at[d, s, i], at_z(1 - 2 * d)
        )

    def live(d, k, j):
        return k < HALF - 1 or (j < CHUNKS // 2) == (d == 0)

    def block(g, r):
        return slice(STARTS[g] + r * ROWS[g], STARTS[g] + (r + 1) * ROWS[g])

    def group(g):
        return slice(STARTS[g], STARTS[g] + X * ROWS[g])

    def x1_copy(g, r):
        rows = block(g, r)
        return remote(st1.at[rows], arr.at[rows], x1_s.at[g, r], x1_r.at[g, r], at_x(r))

    def x2_copy(g, i, r):
        rows = block(g, r)
        return remote(
            st2.at[i, rows], br.at[i, rows], x2_s.at[g, i, r], x2_r.at[g, i, r], at_x(-r)
        )

    def x3_copy(g, i, r):
        rows = block(g, r)
        return remote(st3.at[i, rows], rr.at[i, rows], x3_s.at[g, i, r], x3_r.at[g, i, r], at_x(r))

    def wrows(y):
        return pl.ds(pl.multiple_of((y * 2 + ci) * drows, drows), drows)

    w_refs = (wg_ref, wu_ref, wd_ref)

    def w_copy(m, r):
        return remote(
            w_refs[m], wf.at[m, wrows(yi)], w_ss.at[m, r - 1], w_rs.at[m, r - 1], at_y(r)
        )

    def f_copy(m, r):
        if r == 0:
            return remote(w_refs[m], wf.at[m, wrows(yi)], f_ss.at[m, r], f_rs.at[m, r], sibling)
        rows = wrows(lax.rem(yi - r + Y, Y))
        return remote(wf.at[m, rows], wf.at[m, rows], f_ss.at[m, r], f_rs.at[m, r], sibling)

    def w_local(m):
        return pltpu.make_async_copy(w_refs[m], wf.at[m, wrows(yi)], w_loc.at[m])

    def share_weight(m):
        for r in (1, 3, 2):
            w_copy(m, r).wait_recv()
            go(f_copy(m, r))

    def finish_weight(m):
        w_local(m).wait()
        for r in range(Y):
            f_copy(m, r).wait_recv()

    lane = lax.broadcasted_iota(jnp.int32, (1, PAIR), 1)
    upper_row = lax.broadcasted_iota(jnp.int32, (PAIR, PAIR), 0)
    upper_col = lax.broadcasted_iota(jnp.int32, (PAIR, PAIR), 1)
    before = (upper_row < upper_col) & ((upper_row < TOK) == (upper_col < TOK))
    before = before.astype(F32).astype(BF16)

    def route(k, spot):
        if k == 0:
            first, second = tab_ref[...], tb[0, HALF - 1]
        else:
            first, second = tb[0, k - 1], tb[1, k - 1]
        table = jnp.where(lane < TOK, first, second)
        gates, names = table[:8], table[8:]
        count, weight = [], []
        for r in range(X):
            expert = (zi * X + lax.rem(xi + r, X)).astype(F32)
            match = names == expert
            count.append(jnp.sum(jnp.where(match, 1.0, 0.0), axis=0, keepdims=True))
            weight.append(jnp.sum(jnp.where(match, gates, 0.0), axis=0, keepdims=True))
        fill = jnp.zeros((8 - X, PAIR), F32)
        count = jnp.concatenate(count + [fill], axis=0)
        slot = dot(count.astype(BF16), before)
        base = jnp.where(lane < TOK, 2 * CAP * spot, 2 * CAP * spot + CAP).astype(F32)
        qs[k] = jnp.where(count > 0.0, slot + base, -1.0)
        ws[k] = jnp.concatenate(weight + [fill], axis=0)

    def tables(g):
        rows = ROWS[g]
        for spot, k in enumerate(GROUPS[g]):
            cols = slice(spot * PAIR, (spot + 1) * PAIR)
            number = lax.broadcasted_iota(jnp.int32, (rows, PAIR), 0).astype(F32)
            parts = []
            for r in range(X):
                hit = number == qs[k][r : r + 1]
                here = slice(r * rows, (r + 1) * rows)
                pm[g][here, cols] = jnp.where(hit, 1.0, 0.0).astype(BF16)
                weighted = jnp.where(hit, ws[k][r : r + 1], 0.0)
                gm[g][here, cols] = weighted.astype(BF16)
                parts.append(weighted)
            gt[g][cols, :] = jnp.concatenate(parts, axis=0).T.astype(BF16)

    def tokens_of(k, j):
        cols = slice(j * cw, (j + 1) * cw)
        if k == 0:
            return [tok_ref[:, cols], zb1[0 if j < CHUNKS // 2 else 1, HALF - 1, j]]
        return [zb1[0, k - 1, j], zb1[1, k - 1, j]]

    def select(g):
        for j in range(CHUNKS):
            cols = slice(j * cw, (j + 1) * cw)
            source = jnp.concatenate([t for k in GROUPS[g] for t in tokens_of(k, j)], axis=0)
            picked = dot(pm[g][...], source).astype(BF16)
            arr[block(g, 0), cols] = picked[: ROWS[g]]
            st1[STARTS[g] + ROWS[g] : STARTS[g] + X * ROWS[g], cols] = picked[ROWS[g] :]
        for r in (2, 1, 3):
            go(x1_copy(g, r))

    def hide(g):
        for r in (2, 1, 3):
            x1_copy(g, r).wait_recv()

        def tile(n, _):
            cols = pl.ds(pl.multiple_of(n * 256, 256), 256)
            gate = dot(arr[group(g), :], wf[0, :, cols])
            up = dot(arr[group(g), :], wf[1, :, cols])
            hid[group(g), cols] = (gate / (1.0 + jnp.exp(-gate)) * up).astype(BF16)
            return 0

        lax.fori_loop(0, hid.shape[1] // 256, tile, 0)

    for m in range(3):
        w_local(m).start()
    for j in range(CHUNKS):
        for d in range(2):
            if j == 0:
                go(t_copy(d, 0))
            go(z1_copy(d, 0, j))
    for m in range(3):
        for r in (1, 3, 2):
            go(w_copy(m, r))
        go(f_copy(m, 0))

    for k in range(1, HALF + 1):
        for j in range(CHUNKS):
            for d in range(2):
                if j == 0 and (k < HALF or d == 0):
                    t_copy(d, k - 1).wait_recv()
                    if k < HALF - 1 or (k == HALF - 1 and d == 0):
                        go(t_copy(d, k))
                if live(d, k - 1, j):
                    z1_copy(d, k - 1, j).wait_recv()
                if k < HALF and live(d, k, j):
                    go(z1_copy(d, k, j))
        pair = k % HALF
        for g, members in enumerate(GROUPS):
            if pair in members:
                route(pair, members.index(pair))
                if pair == members[-1]:
                    tables(g)
                    select(g)
        if k == 4:
            share_weight(0)
        if k == 7:
            share_weight(1)
            finish_weight(0)
            finish_weight(1)
            hide(0)
    hide(1)
    share_weight(2)
    hide(2)
    finish_weight(2)

    def place(i):
        return lax.rem(yi + 1 + i, CHUNKS)

    def back(g, i):
        rows = pl.ds(pl.multiple_of(place(i) * cw, cw), cw)
        made = dot(hid[group(g), :], wf[2, rows, :], ((1,), (1,))).astype(BF16)
        br[i, block(g, 0)] = made[: ROWS[g]]
        st2[i, STARTS[g] + ROWS[g] : STARTS[g] + X * ROWS[g]] = made[ROWS[g] :]
        for r in (2, 1, 3):
            go(x2_copy(g, i, r))

    def share(k, i):
        for g, members in enumerate(GROUPS):
            if k in members:
                spot = members.index(k)
                return dot(gt[g][spot * PAIR : (spot + 1) * PAIR, :], br[i, group(g)])

    order = len(GROUPS) - 1

    def reduce_step(i, s):
        if s in (0, 2, 5):
            g = {0: 2, 2: 1, 5: 0}[s]
            for r in (2, 1, 3):
                x2_copy(g, i, r).wait_recv()
        part = share((HALF - s) % HALF, i)
        if s == 0:
            d = 0 if i < CHUNKS // 2 else 1
            rs_s[d, 0, i] = part[TOK:].astype(BF16)
            go(rs_copy(d, 0, i))
            own[i] = part[:TOK]
            back(1, i)
        else:
            for d in range(2):
                mine = part[TOK:] if d == 0 else part[:TOK]
                if s > 1 or live(d, HALF - 1, i):
                    rs_copy(d, s - 1, i).wait_recv()
                    mine = mine + rs_r[d, s - 1, i].astype(F32)
                rs_s[d, s, i] = mine.astype(BF16)
                go(rs_copy(d, s, i))
            if s == 1:
                back(0, i)

    def finish_tangent(i):
        cols = pl.ds(pl.multiple_of(place(i) * cw, cw), cw)
        total = own[i]
        for d in range(2):
            rs_copy(d, HALF - 1, i).wait_recv()
            total = total + rs_r[d, HALF - 1, i].astype(F32)
        tan_ref[:, cols] = total
        sc[i] = (curv_ref[:, cols].astype(F32) * total).astype(BF16)
        for d in range(2):
            go(z3_copy(d, 0, i))

    def scaled_of(k, i):
        if k == 0:
            return [sc[i], zb3[0 if i < CHUNKS // 2 else 1, HALF - 1, i]]
        return [zb3[0, k - 1, i], zb3[1, k - 1, i]]

    def gather_step(i, k):
        for d in range(2):
            if live(d, k - 1, i):
                z3_copy(d, k - 1, i).wait_recv()
            if k < HALF and live(d, k, i):
                go(z3_copy(d, k, i))
        for g, members in enumerate(GROUPS):
            if k % HALF == members[-1]:
                source = jnp.concatenate([t for m in members for t in scaled_of(m, i)], axis=0)
                picked = dot(gm[g][...], source).astype(BF16)
                rr[i, block(g, 0)] = picked[: ROWS[g]]
                st3[i, STARTS[g] + ROWS[g] : STARTS[g] + X * ROWS[g]] = picked[ROWS[g] :]
                for r in (2, 1, 3):
                    go(x3_copy(g, i, r))

    hw = cw // 2
    held = []

    def multiply(i):
        for g in range(len(GROUPS)):
            for r in (2, 1, 3):
                x3_copy(g, i, r).wait_recv()
        theirs = pl.ds(pl.multiple_of((1 - ci) * hw, hw), hw)
        mine = pl.ds(pl.multiple_of(ci * hw, hw), hw)
        ps[i] = dot(rr[i, :, theirs], hid[...], ((0,), (0,))).astype(BF16)
        go(remote(ps.at[i], pr.at[i], p_s.at[i], p_r.at[i], sibling))
        out_ref[...] = dot(rr[i, :, mine], hid[...], ((0,), (0,)))
        remote(ps.at[i], pr.at[i], p_s.at[i], p_r.at[i], sibling).wait_recv()
        total = out_ref[...] + pr[i].astype(F32)
        if i < Y - 1:
            ys[i] = total.astype(BF16)
            go(remote(ys.at[i], yr.at[i], y_s.at[i], y_r.at[i], at_y(1 + i)))
        else:
            for n in range(Y - 1):
                remote(ys.at[n], yr.at[n], y_s.at[n], y_r.at[n], at_y(1 + n)).wait_recv()
                total = total + yr[n].astype(F32)
            out_ref[...] = total

    for i in range(CHUNKS):
        back(2, i)
    for tick in range(2 * HALF + 2 + LAG * (CHUNKS - 1)):
        for i in range(CHUNKS):
            u = tick - LAG * i
            if 0 <= u < HALF:
                reduce_step(i, u)
            elif u == HALF:
                finish_tangent(i)
            elif HALF < u <= 2 * HALF:
                gather_step(i, u - HALF)
            elif u == 2 * HALF + 1:
                multiply(i)

    for copy in sends:
        copy.wait_send()


def per_device(activations, curvature, routes, route_gates, w_gate, w_up, v_down):
    tokens, width = activations.shape
    features, hidden = w_gate.shape[1:]
    cw = width // CHUNKS
    table = jnp.concatenate([route_gates.T, routes.T.astype(F32)], axis=0)
    table = jnp.concatenate([table, table], axis=1)
    vmem = pl.BlockSpec(memory_space=pltpu.VMEM)
    hbm = pl.BlockSpec(memory_space=pl.ANY)
    dma = pltpu.SemaphoreType.DMA
    n = len(GROUPS)
    scratch = [
        pltpu.VMEM((3, width, hidden), BF16),
        pltpu.VMEM((2, HALF, CHUNKS, tokens, cw), BF16),
        pltpu.VMEM((2, HALF) + table.shape, F32),
        pltpu.VMEM((HALF, 8, PAIR), F32),
        pltpu.VMEM((HALF, 8, PAIR), F32),
    ]
    scratch += [pltpu.VMEM((X * ROWS[g], PAIR * len(GROUPS[g])), BF16) for g in range(n)] * 2
    scratch += [pltpu.VMEM((PAIR * len(GROUPS[g]), X * ROWS[g]), BF16) for g in range(n)]
    scratch += [
        pltpu.VMEM((TOTAL, width), BF16),
        pltpu.VMEM((TOTAL, width), BF16),
        pltpu.VMEM((TOTAL, hidden), BF16),
        pltpu.VMEM((CHUNKS, TOTAL, cw), BF16),
        pltpu.VMEM((CHUNKS, TOTAL, cw), BF16),
        pltpu.VMEM((2, HALF, CHUNKS, tokens, cw), BF16),
        pltpu.VMEM((2, HALF, CHUNKS, tokens, cw), BF16),
        pltpu.VMEM((CHUNKS, tokens, cw), BF16),
        pltpu.VMEM((2, HALF, CHUNKS, tokens, cw), BF16),
        pltpu.VMEM((CHUNKS, TOTAL, cw), BF16),
        pltpu.VMEM((CHUNKS, TOTAL, cw), BF16),
        pltpu.VMEM((CHUNKS, tokens, cw), F32),
        pltpu.VMEM((CHUNKS, features, hidden), BF16),
        pltpu.VMEM((CHUNKS, features, hidden), BF16),
        pltpu.VMEM((Y - 1, features, hidden), BF16),
        pltpu.VMEM((Y - 1, features, hidden), BF16),
        dma((3,)),
        dma((3, Y - 1)), dma((3, Y - 1)),
        dma((3, Y)), dma((3, Y)),
        dma((2, HALF, CHUNKS)), dma((2, HALF, CHUNKS)),
        dma((2, HALF)), dma((2, HALF)),
        dma((n, X)), dma((n, X)),
        dma((n, CHUNKS, X)), dma((n, CHUNKS, X)),
        dma((2, HALF, CHUNKS)), dma((2, HALF, CHUNKS)),
        dma((2, HALF, CHUNKS)), dma((2, HALF, CHUNKS)),
        dma((n, CHUNKS, X)), dma((n, CHUNKS, X)),
        dma((CHUNKS,)), dma((CHUNKS,)),
        dma((Y - 1,)), dma((Y - 1,)),
    ]
    tangent, product = pl.pallas_call(
        kernel,
        out_shape=(
            jax.ShapeDtypeStruct((tokens, width), F32),
            jax.ShapeDtypeStruct((features, hidden), F32),
        ),
        in_specs=[vmem, vmem, vmem, hbm, hbm, hbm],
        out_specs=(vmem, vmem),
        scratch_shapes=scratch,
        compiler_params=pltpu.CompilerParams(
            collective_id=0, has_side_effects=True, vmem_limit_bytes=62 * 2**20
        ),
    )(activations, curvature, table, w_gate[0], w_up[0], v_down[0])
    return (tangent, product[None])


def solution(mesh):
    return jax.shard_map(
        per_device,
        mesh=mesh,
        in_specs=(
            P(("dp", "expert"), None),
            P(("dp", "expert"), None),
            P(("dp", "expert"), None),
            P(("dp", "expert"), None),
            P("expert", "dp", None),
            P("expert", "dp", None),
            P("expert", "dp", None),
        ),
        out_specs=(P(("dp", "expert"), None), P("expert", "dp", None)),
        check_vma=False,
    )
```

```python
import functools

import jax
import jax.numpy as jnp
from jax import lax
from jax.experimental import pallas as pl
from jax.experimental.pallas import tpu as pltpu
from jax.sharding import PartitionSpec as P

X = 4
Y = 4
HALF = 8
TOK = 64
CAP = 9
CHUNKS = 4
PAIR = 2 * TOK
OWN, FAR = 0, HALF
BOUNDS = (0, 48, 80, 112, 128, 144)


def many(k):
    return 1 if k in (OWN, FAR) else 2


def first_row(k):
    return 0 if k == OWN else CAP * (2 * k - 1)


GROUPS = tuple(
    tuple(
        k
        for k in range(HALF + 1)
        if first_row(k) < hi and first_row(k) + CAP * many(k) > lo
    )
    for lo, hi in zip(BOUNDS, BOUNDS[1:])
)
COLS = tuple(TOK * sum(many(k) for k in g) for g in GROUPS)
ROWS = tuple(hi - lo for lo, hi in zip(BOUNDS, BOUNDS[1:]))
STARTS = tuple(X * sum(ROWS[:g]) for g in range(len(GROUPS)))
TOTAL = X * sum(ROWS)
LAG = 2
MESH = pl.DeviceIdType.MESH
F32 = jnp.float32
BF16 = jnp.bfloat16


def dot(a, b, dims=((1,), (0,))):
    return lax.dot_general(a, b, (dims, ((), ())), preferred_element_type=F32)


def kernel(
    tok_ref, curv_ref, tab_ref, wg_ref, wu_ref, wd_ref, tan_ref, out_ref,
    wf, zb1, tb, qs, ws, pm0, pm1, pm2, pm3, pm4, gm0, gm1, gm2, gm3, gm4, gt0, gt1, gt2, gt3, gt4,
    st1, arr, hid, st2, br, rs_s, rs_r, sc, zb3, st3, rr, own, ps, pr, ys, yr, half, tok_v, curv_v,
    in_s, w_loc, w_ss, w_rs, r_ss, r_rs, f_ss, f_rs, z1_s, z1_r, t_s, t_r, x1_s, x1_r, x2_s, x2_r,
    rs_ss, rs_rs, z3_s, z3_r, x3_s, x3_r, p_s, p_r, y_s, y_r,
):
    pm = (pm0, pm1, pm2, pm3, pm4)
    gm = (gm0, gm1, gm2, gm3, gm4)
    gt = (gt0, gt1, gt2, gt3, gt4)
    dp = lax.axis_index("dp")
    e = lax.axis_index("expert")
    zi, xi = e // X, lax.rem(e, X)
    yi, ci = dp // 2, lax.rem(dp, 2)
    width = tok_ref.shape[1]
    cw = width // CHUNKS
    drows = wg_ref.shape[0]
    experts = 4 * HALF * 2

    def at_z(step):
        return (dp, lax.rem(e + step * X + experts, experts))

    def at_x(step):
        return (dp, zi * X + lax.rem(xi + step + X, X))

    def at_y(step):
        return (lax.rem(yi + step + Y, Y) * 2 + ci, e)

    sibling = (yi * 2 + (1 - ci), e)
    sends = []

    def remote(src, dst, ss, rs, dev):
        return pltpu.make_async_remote_copy(
            src_ref=src, dst_ref=dst, send_sem=ss, recv_sem=rs, device_id=dev, device_id_type=MESH
        )

    def go(copy):
        copy.start()
        sends.append(copy)

    loads = [
        pltpu.make_async_copy(tok_ref, tok_v, in_s.at[0]),
        pltpu.make_async_copy(curv_ref, curv_v, in_s.at[1]),
    ]
    for load in loads:
        load.start()
    barrier = pltpu.get_barrier_semaphore()
    partners = [at_z(1), at_z(-1), at_x(1), at_x(2), at_x(3), at_y(1), at_y(2), at_y(3), sibling]
    for dev in partners:
        pl.semaphore_signal(barrier, inc=1, device_id=dev, device_id_type=MESH)
    pl.semaphore_wait(barrier, len(partners))
    for load in loads:
        load.wait()

    def z1_copy(d, k, j):
        src = tok_v.at[:, j * cw : (j + 1) * cw] if k == 0 else zb1.at[d, k - 1, j]
        return remote(src, zb1.at[d, k, j], z1_s.at[d, k, j], z1_r.at[d, k, j], at_z(1 - 2 * d))

    def t_copy(d, k):
        src = tab_ref if k == 0 else tb.at[d, k - 1]
        return remote(src, tb.at[d, k], t_s.at[d, k], t_r.at[d, k], at_z(1 - 2 * d))

    def z3_copy(d, k, i):
        src = sc.at[i] if k == 0 else zb3.at[d, k - 1, i]
        return remote(src, zb3.at[d, k, i], z3_s.at[d, k, i], z3_r.at[d, k, i], at_z(1 - 2 * d))

    def rs_copy(d, s, i):
        return remote(
            rs_s.at[d, s, i], rs_r.at[d, s, i], rs_ss.at[d, s, i], rs_rs.at[d, s, i], at_z(1 - 2 * d)
        )

    def live(d, k, j):
        return k < HALF - 1 or (j < CHUNKS // 2) == (d == 0)

    def block(g, r):
        return slice(STARTS[g] + r * ROWS[g], STARTS[g] + (r + 1) * ROWS[g])

    def group(g, last=None):
        last = g if last is None else last
        return slice(STARTS[g], STARTS[last] + X * ROWS[last])

    def x1_copy(g, r):
        rows = block(g, r)
        return remote(st1.at[rows], arr.at[rows], x1_s.at[g, r], x1_r.at[g, r], at_x(r))

    def x2_copy(g, i, r):
        rows = block(g, r)
        return remote(
            st2.at[i, rows], br.at[i, rows], x2_s.at[g, i, r], x2_r.at[g, i, r], at_x(-r)
        )

    def x3_copy(g, i, r):
        rows = block(g, r)
        return remote(st3.at[i, rows], rr.at[i, rows], x3_s.at[g, i, r], x3_r.at[g, i, r], at_x(r))

    def wrows(y):
        return pl.ds(pl.multiple_of((y * 2 + ci) * drows, drows), drows)

    w_refs = (wg_ref, wu_ref, wd_ref)

    def w_copy(m, r):
        return remote(
            w_refs[m], wf.at[m, wrows(yi)], w_ss.at[m, r // 2], w_rs.at[m, r // 2], at_y(r)
        )

    def relay_copy(m, h):
        y = lax.rem(yi + Y - 1 + 2 * h, Y)
        start = (y * 2 + ci) * drows + h * (drows // 2)
        rows = pl.ds(pl.multiple_of(start, drows // 2), drows // 2)
        return remote(
            wf.at[m, rows], wf.at[m, rows], r_ss.at[m, h], r_rs.at[m, h], at_y(1 - 2 * h)
        )

    def f_copy(m, r):
        if r == 0:
            return remote(w_refs[m], wf.at[m, wrows(yi)], f_ss.at[m, r], f_rs.at[m, r], sibling)
        rows = wrows(lax.rem(yi - r + Y, Y))
        return remote(wf.at[m, rows], wf.at[m, rows], f_ss.at[m, r], f_rs.at[m, r], sibling)

    def w_local(m):
        return pltpu.make_async_copy(w_refs[m], wf.at[m, wrows(yi)], w_loc.at[m])

    def relay_weight(m):
        for h, r in enumerate((1, 3)):
            w_copy(m, r).wait_recv()
            go(relay_copy(m, h))
        for r in (1, 3):
            go(f_copy(m, r))

    def share_weight(m):
        for h in range(2):
            relay_copy(m, h).wait_recv()
        go(f_copy(m, 2))

    def finish_weight(m):
        w_local(m).wait()
        for r in range(Y):
            f_copy(m, r).wait_recv()

    lane = lax.broadcasted_iota(jnp.int32, (1, PAIR), 1)
    upper_row = lax.broadcasted_iota(jnp.int32, (PAIR, PAIR), 0)
    upper_col = lax.broadcasted_iota(jnp.int32, (PAIR, PAIR), 1)
    before = (upper_row < upper_col) & ((upper_row < TOK) == (upper_col < TOK))
    before = before.astype(F32).astype(BF16)

    def spot(g, k):
        members = GROUPS[g]
        start = TOK * sum(many(m) for m in members[: members.index(k)])
        return slice(start, start + many(k) * TOK)

    def route(k):
        first = second = tab_ref[...]
        if k == FAR:
            first = tb[0, HALF - 1]
        elif k != OWN:
            first, second = tb[0, k - 1], tb[1, k - 1]
        gates = jnp.where(lane < TOK, first, pltpu.roll(second, TOK, axis=1))
        names = jnp.where(lane < TOK, pltpu.roll(first, TOK, axis=1), second)
        count, weight = [], []
        for r in range(X):
            expert = (zi * X + lax.rem(xi + r, X)).astype(F32)
            match = names == expert
            count.append(jnp.sum(jnp.where(match, 1.0, 0.0), axis=0, keepdims=True))
            weight.append(jnp.sum(jnp.where(match, gates, 0.0), axis=0, keepdims=True))
        fill = jnp.zeros((8 - X, PAIR), F32)
        count = jnp.concatenate(count + [fill], axis=0)
        slot = dot(count.astype(BF16), before)
        base = jnp.where(lane < TOK, first_row(k), first_row(k) + CAP).astype(F32)
        qs[k] = jnp.where(count > 0.0, slot + base, -1.0)
        ws[k] = jnp.concatenate(weight + [fill], axis=0)

    def tables(g):
        rows = ROWS[g]
        number = (lax.broadcasted_iota(jnp.int32, (rows, PAIR), 0) + BOUNDS[g]).astype(F32)
        for k in GROUPS[g]:
            cols, size = spot(g, k), many(k) * TOK
            parts = []
            for r in range(X):
                hit = number == qs[k][r : r + 1]
                here = slice(r * rows, (r + 1) * rows)
                pm[g][here, cols] = jnp.where(hit, 1.0, 0.0).astype(BF16)[:, :size]
                weighted = jnp.where(hit, ws[k][r : r + 1], 0.0)
                gm[g][here, cols] = weighted.astype(BF16)[:, :size]
                parts.append(weighted)
            gt[g][cols, :] = jnp.concatenate(parts, axis=0).T.astype(BF16)[:size]

    def tokens_of(k, j):
        cols = slice(j * cw, (j + 1) * cw)
        if k == OWN:
            return [tok_v[:, cols]]
        if k == FAR:
            return [zb1[0 if j < CHUNKS // 2 else 1, HALF - 1, j]]
        return [zb1[0, k - 1, j], zb1[1, k - 1, j]]

    def select(g):
        for j in range(CHUNKS):
            cols = slice(j * cw, (j + 1) * cw)
            source = jnp.concatenate([t for k in GROUPS[g] for t in tokens_of(k, j)], axis=0)
            picked = dot(pm[g][...], source).astype(BF16)
            arr[block(g, 0), cols] = picked[: ROWS[g]]
            st1[STARTS[g] + ROWS[g] : STARTS[g] + X * ROWS[g], cols] = picked[ROWS[g] :]
        for r in (2, 1, 3):
            go(x1_copy(g, r))

    def hide(g, last):
        for n in range(g, last + 1):
            for r in (2, 1, 3):
                x1_copy(n, r).wait_recv()

        def tile(n, _):
            cols = pl.ds(pl.multiple_of(n * 256, 256), 256)
            gate = dot(arr[group(g, last), :], wf[0, :, cols])
            up = dot(arr[group(g, last), :], wf[1, :, cols])
            hid[group(g, last), cols] = (gate / (1.0 + jnp.exp(-gate)) * up).astype(BF16)
            return 0

        lax.fori_loop(0, hid.shape[1] // 256, tile, 0)

    for m in range(3):
        w_local(m).start()
    for j in range(CHUNKS):
        for d in range(2):
            if j == 0:
                go(t_copy(d, 0))
            go(z1_copy(d, 0, j))
    for m in range(3):
        for r in (1, 3):
            go(w_copy(m, r))
        go(f_copy(m, 0))

    route(OWN)
    for k in range(1, HALF + 1):
        for j in range(CHUNKS):
            for d in range(2):
                if j == 0 and (k < HALF or d == 0):
                    t_copy(d, k - 1).wait_recv()
                    if k < HALF - 1 or (k == HALF - 1 and d == 0):
                        go(t_copy(d, k))
                if live(d, k - 1, j):
                    z1_copy(d, k - 1, j).wait_recv()
                if k < HALF and live(d, k, j):
                    go(z1_copy(d, k, j))
        route(k)
        for g, members in enumerate(GROUPS):
            if k == max(members):
                tables(g)
                select(g)
        if k in (2, 3, 5):
            relay_weight({2: 0, 3: 1, 5: 2}[k])
        if k in (5, 6):
            share_weight(k - 5)
    finish_weight(0)
    finish_weight(1)
    hide(0, 2)
    share_weight(2)
    hide(3, 4)
    finish_weight(2)

    def place(i):
        return lax.rem(yi + 1 + i, CHUNKS)

    def back(g, last, i):
        rows = pl.ds(pl.multiple_of(place(i) * cw, cw), cw)
        made = dot(hid[group(g, last), :], wf[2, rows, :], ((1,), (1,))).astype(BF16)
        for n in range(last, g - 1, -1):
            start = STARTS[n] - STARTS[g]
            br[i, block(n, 0)] = made[start : start + ROWS[n]]
            rest = slice(STARTS[n] + ROWS[n], STARTS[n] + X * ROWS[n])
            st2[i, rest] = made[start + ROWS[n] : start + X * ROWS[n]]
            for r in (2, 1, 3):
                go(x2_copy(n, i, r))

    arrived = set()

    def share(k, i):
        total = None
        for g, members in enumerate(GROUPS):
            if k in members:
                if (g, i) not in arrived:
                    arrived.add((g, i))
                    for r in (2, 1, 3):
                        x2_copy(g, i, r).wait_recv()
                part = dot(gt[g][spot(g, k), :], br[i, group(g)])
                total = part if total is None else total + part
        return total

    def reduce_step(i, s):
        part = share(HALF - s, i)
        if s == 0:
            d = 0 if i < CHUNKS // 2 else 1
            rs_s[d, 0, i] = part.astype(BF16)
            go(rs_copy(d, 0, i))
            back(2, 2, i)
        else:
            for d in range(2):
                mine = part[TOK:] if d == 0 else part[:TOK]
                if s > 1 or live(d, HALF - 1, i):
                    rs_copy(d, s - 1, i).wait_recv()
                    mine = mine + rs_r[d, s - 1, i].astype(F32)
                rs_s[d, s, i] = mine.astype(BF16)
                go(rs_copy(d, s, i))
            if s in (1, 2):
                back(2 - s, 2 - s, i)
            if s == 6:
                own[i] = share(OWN, i)

    def finish_tangent(i):
        cols = pl.ds(pl.multiple_of(place(i) * cw, cw), cw)
        total = own[i]
        for d in range(2):
            rs_copy(d, HALF - 1, i).wait_recv()
            total = total + rs_r[d, HALF - 1, i].astype(F32)
        tan_ref[:, cols] = total
        sc[i] = (curv_v[:, cols].astype(F32) * total).astype(BF16)
        for d in range(2):
            go(z3_copy(d, 0, i))

    def scaled_of(k, i):
        if k == OWN:
            return [sc[i]]
        if k == FAR:
            return [zb3[0 if i < CHUNKS // 2 else 1, HALF - 1, i]]
        return [zb3[0, k - 1, i], zb3[1, k - 1, i]]

    def gather_step(i, k):
        for d in range(2):
            if live(d, k - 1, i):
                z3_copy(d, k - 1, i).wait_recv()
            if k < HALF and live(d, k, i):
                go(z3_copy(d, k, i))
        for g, members in enumerate(GROUPS):
            if k == max(members):
                source = jnp.concatenate([t for m in members for t in scaled_of(m, i)], axis=0)
                picked = dot(gm[g][...], source).astype(BF16)
                rr[i, block(g, 0)] = picked[: ROWS[g]]
                st3[i, STARTS[g] + ROWS[g] : STARTS[g] + X * ROWS[g]] = picked[ROWS[g] :]
                for r in (2, 1, 3):
                    go(x3_copy(g, i, r))

    hw = cw // 2

    def pair_copy(i):
        return remote(ps.at[i], pr.at[i], p_s.at[i], p_r.at[i], sibling)

    def home_copy(i):
        return remote(ys.at[i], yr.at[i], y_s.at[i], y_r.at[i], at_y(1 + i))

    def multiply(i):
        for g in range(len(GROUPS)):
            for r in (2, 1, 3):
                x3_copy(g, i, r).wait_recv()
        theirs = pl.ds(pl.multiple_of((1 - ci) * hw, hw), hw)
        mine = pl.ds(pl.multiple_of(ci * hw, hw), hw)
        ps[i] = dot(rr[i, :, theirs], hid[...], ((0,), (0,))).astype(BF16)
        go(pair_copy(i))
        half[i % 2] = dot(rr[i, :, mine], hid[...], ((0,), (0,)))

    def send_home(i):
        pair_copy(i).wait_recv()
        total = half[i % 2] + pr[i].astype(F32)
        if i < Y - 1:
            ys[i] = total.astype(BF16)
            go(home_copy(i))
        else:
            for n in range(Y - 1):
                home_copy(n).wait_recv()
                total = total + yr[n].astype(F32)
            out_ref[...] = total

    for i in range(CHUNKS):
        back(3, 4, i)
    for tick in range(2 * HALF + 3 + LAG * (CHUNKS - 1)):
        for i in range(CHUNKS):
            u = tick - LAG * i
            if 0 <= u < HALF:
                reduce_step(i, u)
            elif u == HALF:
                finish_tangent(i)
            elif HALF < u <= 2 * HALF:
                gather_step(i, u - HALF)
            elif u == 2 * HALF + 1:
                multiply(i)
            elif u == 2 * HALF + 2:
                send_home(i)

    for copy in sends:
        copy.wait_send()


def per_device(activations, curvature, routes, route_gates, w_gate, w_up, v_down):
    tokens, width = activations.shape
    features, hidden = w_gate.shape[1:]
    cw = width // CHUNKS
    table = jnp.concatenate([route_gates.T, routes.T.astype(F32)], axis=1)
    vmem = pl.BlockSpec(memory_space=pltpu.VMEM)
    hbm = pl.BlockSpec(memory_space=pl.ANY)
    dma = pltpu.SemaphoreType.DMA
    n = len(GROUPS)
    scratch = [
        pltpu.VMEM((3, width, hidden), BF16),
        pltpu.VMEM((2, HALF, CHUNKS, tokens, cw), BF16),
        pltpu.VMEM((2, HALF) + table.shape, F32),
        pltpu.VMEM((HALF + 1, 8, PAIR), F32),
        pltpu.VMEM((HALF + 1, 8, PAIR), F32),
    ]
    scratch += [pltpu.VMEM((X * ROWS[g], COLS[g]), BF16) for g in range(n)] * 2
    scratch += [pltpu.VMEM((COLS[g], X * ROWS[g]), BF16) for g in range(n)]
    scratch += [
        pltpu.VMEM((TOTAL, width), BF16),
        pltpu.VMEM((TOTAL, width), BF16),
        pltpu.VMEM((TOTAL, hidden), BF16),
        pltpu.VMEM((CHUNKS, TOTAL, cw), BF16),
        pltpu.VMEM((CHUNKS, TOTAL, cw), BF16),
        pltpu.VMEM((2, HALF, CHUNKS, tokens, cw), BF16),
        pltpu.VMEM((2, HALF, CHUNKS, tokens, cw), BF16),
        pltpu.VMEM((CHUNKS, tokens, cw), BF16),
        pltpu.VMEM((2, HALF, CHUNKS, tokens, cw), BF16),
        pltpu.VMEM((CHUNKS, TOTAL, cw), BF16),
        pltpu.VMEM((CHUNKS, TOTAL, cw), BF16),
        pltpu.VMEM((CHUNKS, tokens, cw), F32),
        pltpu.VMEM((CHUNKS, features, hidden), BF16),
        pltpu.VMEM((CHUNKS, features, hidden), BF16),
        pltpu.VMEM((Y - 1, features, hidden), BF16),
        pltpu.VMEM((Y - 1, features, hidden), BF16),
        pltpu.VMEM((2, features, hidden), F32),
        pltpu.VMEM((tokens, width), BF16),
        pltpu.VMEM((tokens, width), BF16),
        dma((2,)),
        dma((3,)),
        dma((3, 2)), dma((3, 2)),
        dma((3, 2)), dma((3, 2)),
        dma((3, Y)), dma((3, Y)),
        dma((2, HALF, CHUNKS)), dma((2, HALF, CHUNKS)),
        dma((2, HALF)), dma((2, HALF)),
        dma((n, X)), dma((n, X)),
        dma((n, CHUNKS, X)), dma((n, CHUNKS, X)),
        dma((2, HALF, CHUNKS)), dma((2, HALF, CHUNKS)),
        dma((2, HALF, CHUNKS)), dma((2, HALF, CHUNKS)),
        dma((n, CHUNKS, X)), dma((n, CHUNKS, X)),
        dma((CHUNKS,)), dma((CHUNKS,)),
        dma((Y - 1,)), dma((Y - 1,)),
    ]
    tangent, product = pl.pallas_call(
        kernel,
        out_shape=(
            jax.ShapeDtypeStruct((tokens, width), F32),
            jax.ShapeDtypeStruct((features, hidden), F32),
        ),
        in_specs=[hbm, hbm, vmem, hbm, hbm, hbm],
        out_specs=(vmem, vmem),
        scratch_shapes=scratch,
        compiler_params=pltpu.CompilerParams(
            collective_id=0, has_side_effects=True, vmem_limit_bytes=62 * 2**20
        ),
    )(activations, curvature, table, w_gate[0], w_up[0], v_down[0])
    return (tangent, product[None])


def solution(mesh):
    return jax.shard_map(
        per_device,
        mesh=mesh,
        in_specs=(
            P(("dp", "expert"), None),
            P(("dp", "expert"), None),
            P(("dp", "expert"), None),
            P(("dp", "expert"), None),
            P("expert", "dp", None),
            P("expert", "dp", None),
            P("expert", "dp", None),
        ),
        out_specs=(P(("dp", "expert"), None), P("expert", "dp", None)),
        check_vma=False,
    )
```

```python
import functools

import jax
import jax.numpy as jnp
from jax import lax
from jax.experimental import pallas as pl
from jax.experimental.pallas import tpu as pltpu
from jax.sharding import PartitionSpec as P

X = 4
Y = 4
HALF = 8
TOK = 64
CAP = 9
CHUNKS = 4
PAIR = 2 * TOK
OWN, FAR = 0, HALF
BOUNDS = (0, 48, 80, 112, 128, 144)


def many(k):
    return 1 if k in (OWN, FAR) else 2


def first_row(k):
    return 0 if k == OWN else CAP * (2 * k - 1)


GROUPS = tuple(
    tuple(
        k
        for k in range(HALF + 1)
        if first_row(k) < hi and first_row(k) + CAP * many(k) > lo
    )
    for lo, hi in zip(BOUNDS, BOUNDS[1:])
)
COLS = tuple(TOK * sum(many(k) for k in g) for g in GROUPS)
ROWS = tuple(hi - lo for lo, hi in zip(BOUNDS, BOUNDS[1:]))
STARTS = tuple(X * sum(ROWS[:g]) for g in range(len(GROUPS)))
TOTAL = X * sum(ROWS)
LAG = 2
MESH = pl.DeviceIdType.MESH
F32 = jnp.float32
BF16 = jnp.bfloat16


def dot(a, b, dims=((1,), (0,))):
    return lax.dot_general(a, b, (dims, ((), ())), preferred_element_type=F32)


def kernel(
    tok_ref, curv_ref, tab_ref, wg_ref, wu_ref, wd_ref, tan_ref, out_ref,
    wf, zb1, tb, qs, ws, pm0, pm1, pm2, pm3, pm4, gm0, gm1, gm2, gm3, gm4, gt0, gt1, gt2, gt3, gt4,
    st1, arr, hid, st2, br, rs_s, rs_r, sc, zb3, st3, rr, own, ps, pr, ys, yr, half, tok_v, curv_v,
    in_s, w_loc, w_ss, w_rs, r_ss, r_rs, f_ss, f_rs, z1_s, z1_r, t_s, t_r, x1_s, x1_r, x2_s, x2_r,
    rs_ss, rs_rs, z3_s, z3_r, x3_s, x3_r, p_s, p_r, y_s, y_r,
):
    pm = (pm0, pm1, pm2, pm3, pm4)
    gm = (gm0, gm1, gm2, gm3, gm4)
    gt = (gt0, gt1, gt2, gt3, gt4)
    dp = lax.axis_index("dp")
    e = lax.axis_index("expert")
    zi, xi = e // X, lax.rem(e, X)
    yi, ci = dp // 2, lax.rem(dp, 2)
    width = tok_ref.shape[1]
    cw = width // CHUNKS
    drows = wg_ref.shape[0]
    experts = 4 * HALF * 2

    def at_z(step):
        return (dp, lax.rem(e + step * X + experts, experts))

    def at_x(step):
        return (dp, zi * X + lax.rem(xi + step + X, X))

    def at_y(step):
        return (lax.rem(yi + step + Y, Y) * 2 + ci, e)

    sibling = (yi * 2 + (1 - ci), e)
    sends = []

    def remote(src, dst, ss, rs, dev):
        return pltpu.make_async_remote_copy(
            src_ref=src, dst_ref=dst, send_sem=ss, recv_sem=rs, device_id=dev, device_id_type=MESH
        )

    def go(copy):
        copy.start()
        sends.append(copy)

    loads = [
        pltpu.make_async_copy(tok_ref, tok_v, in_s.at[0]),
        pltpu.make_async_copy(curv_ref, curv_v, in_s.at[1]),
    ]
    for load in loads:
        load.start()
    barrier = pltpu.get_barrier_semaphore()
    partners = [at_z(1), at_z(-1), at_x(1), at_x(2), at_x(3), at_y(1), at_y(2), at_y(3), sibling]
    for dev in partners:
        pl.semaphore_signal(barrier, inc=1, device_id=dev, device_id_type=MESH)
    pl.semaphore_wait(barrier, len(partners))
    for load in loads:
        load.wait()

    def z1_copy(d, k, j):
        src = tok_v.at[:, j * cw : (j + 1) * cw] if k == 0 else zb1.at[d, k - 1, j]
        return remote(src, zb1.at[d, k, j], z1_s.at[d, k, j], z1_r.at[d, k, j], at_z(1 - 2 * d))

    def t_copy(d, k):
        src = tab_ref if k == 0 else tb.at[d, k - 1]
        return remote(src, tb.at[d, k], t_s.at[d, k], t_r.at[d, k], at_z(1 - 2 * d))

    def z3_copy(d, k, i):
        src = sc.at[i] if k == 0 else zb3.at[d, k - 1, i]
        return remote(src, zb3.at[d, k, i], z3_s.at[d, k, i], z3_r.at[d, k, i], at_z(1 - 2 * d))

    def rs_copy(d, s, i):
        return remote(
            rs_s.at[d, s, i], rs_r.at[d, s, i], rs_ss.at[d, s, i], rs_rs.at[d, s, i], at_z(1 - 2 * d)
        )

    def live(d, k, j):
        return k < HALF - 1 or (j < CHUNKS // 2) == (d == 0)

    def block(g, r):
        return slice(STARTS[g] + r * ROWS[g], STARTS[g] + (r + 1) * ROWS[g])

    def group(g, last=None):
        last = g if last is None else last
        return slice(STARTS[g], STARTS[last] + X * ROWS[last])

    def x1_copy(g, r):
        rows = block(g, r)
        return remote(st1.at[rows], arr.at[rows], x1_s.at[g, r], x1_r.at[g, r], at_x(r))

    def x2_copy(g, i, r):
        rows = block(g, r)
        return remote(
            st2.at[i, rows], br.at[i, rows], x2_s.at[g, i, r], x2_r.at[g, i, r], at_x(-r)
        )

    def x3_copy(g, i, r):
        rows = block(g, r)
        return remote(st3.at[i, rows], rr.at[i, rows], x3_s.at[g, i, r], x3_r.at[g, i, r], at_x(r))

    def wrows(y):
        return pl.ds(pl.multiple_of((y * 2 + ci) * drows, drows), drows)

    w_refs = (wg_ref, wu_ref, wd_ref)

    def w_copy(m, r):
        return remote(
            w_refs[m], wf.at[m, wrows(yi)], w_ss.at[m, r // 2], w_rs.at[m, r // 2], at_y(r)
        )

    def relay_copy(m, h):
        y = lax.rem(yi + Y - 1 + 2 * h, Y)
        start = (y * 2 + ci) * drows + h * (drows // 2)
        rows = pl.ds(pl.multiple_of(start, drows // 2), drows // 2)
        return remote(
            wf.at[m, rows], wf.at[m, rows], r_ss.at[m, h], r_rs.at[m, h], at_y(1 - 2 * h)
        )

    def f_copy(m, r):
        if r == 0:
            return remote(w_refs[m], wf.at[m, wrows(yi)], f_ss.at[m, r], f_rs.at[m, r], sibling)
        rows = wrows(lax.rem(yi - r + Y, Y))
        return remote(wf.at[m, rows], wf.at[m, rows], f_ss.at[m, r], f_rs.at[m, r], sibling)

    def w_local(m):
        return pltpu.make_async_copy(w_refs[m], wf.at[m, wrows(yi)], w_loc.at[m])

    def relay_weight(m):
        for h, r in enumerate((1, 3)):
            w_copy(m, r).wait_recv()
            go(relay_copy(m, h))
        for r in (1, 3):
            go(f_copy(m, r))

    def share_weight(m):
        for h in range(2):
            relay_copy(m, h).wait_recv()
        go(f_copy(m, 2))

    def finish_weight(m):
        w_local(m).wait()
        for r in range(Y):
            f_copy(m, r).wait_recv()

    lane = lax.broadcasted_iota(jnp.int32, (1, PAIR), 1)
    upper_row = lax.broadcasted_iota(jnp.int32, (PAIR, PAIR), 0)
    upper_col = lax.broadcasted_iota(jnp.int32, (PAIR, PAIR), 1)
    before = (upper_row < upper_col) & ((upper_row < TOK) == (upper_col < TOK))
    before = before.astype(F32).astype(BF16)

    def spot(g, k):
        members = GROUPS[g]
        start = TOK * sum(many(m) for m in members[: members.index(k)])
        return slice(start, start + many(k) * TOK)

    def route(k):
        first = second = tab_ref[...]
        if k == FAR:
            first = tb[0, HALF - 1]
        elif k != OWN:
            first, second = tb[0, k - 1], tb[1, k - 1]
        gates = jnp.where(lane < TOK, first, pltpu.roll(second, TOK, axis=1))
        names = jnp.where(lane < TOK, pltpu.roll(first, TOK, axis=1), second)
        count, weight = [], []
        for r in range(X):
            expert = (zi * X + lax.rem(xi + r, X)).astype(F32)
            match = names == expert
            count.append(jnp.sum(jnp.where(match, 1.0, 0.0), axis=0, keepdims=True))
            weight.append(jnp.sum(jnp.where(match, gates, 0.0), axis=0, keepdims=True))
        fill = jnp.zeros((8 - X, PAIR), F32)
        count = jnp.concatenate(count + [fill], axis=0)
        slot = dot(count.astype(BF16), before)
        base = jnp.where(lane < TOK, first_row(k), first_row(k) + CAP).astype(F32)
        qs[k] = jnp.where(count > 0.0, slot + base, -1.0)
        ws[k] = jnp.concatenate(weight + [fill], axis=0)

    def tables(g):
        rows = ROWS[g]
        number = (lax.broadcasted_iota(jnp.int32, (rows, PAIR), 0) + BOUNDS[g]).astype(F32)
        for k in GROUPS[g]:
            cols, size = spot(g, k), many(k) * TOK
            parts = []
            for r in range(X):
                hit = number == qs[k][r : r + 1]
                here = slice(r * rows, (r + 1) * rows)
                pm[g][here, cols] = jnp.where(hit, 1.0, 0.0).astype(BF16)[:, :size]
                weighted = jnp.where(hit, ws[k][r : r + 1], 0.0)
                gm[g][here, cols] = weighted.astype(BF16)[:, :size]
                parts.append(weighted)
            gt[g][cols, :] = jnp.concatenate(parts, axis=0).T.astype(BF16)[:size]

    def tokens_of(k, j):
        cols = slice(j * cw, (j + 1) * cw)
        if k == OWN:
            return [tok_v[:, cols]]
        if k == FAR:
            return [zb1[0 if j < CHUNKS // 2 else 1, HALF - 1, j]]
        return [zb1[0, k - 1, j], zb1[1, k - 1, j]]

    def select(g):
        for j in range(CHUNKS):
            cols = slice(j * cw, (j + 1) * cw)
            source = jnp.concatenate([t for k in GROUPS[g] for t in tokens_of(k, j)], axis=0)
            picked = dot(pm[g][...], source).astype(BF16)
            arr[block(g, 0), cols] = picked[: ROWS[g]]
            st1[STARTS[g] + ROWS[g] : STARTS[g] + X * ROWS[g], cols] = picked[ROWS[g] :]
        for r in (2, 1, 3):
            go(x1_copy(g, r))

    def hide(g, last):
        for n in range(g, last + 1):
            for r in (2, 1, 3):
                x1_copy(n, r).wait_recv()

        def tile(n, _):
            cols = pl.ds(pl.multiple_of(n * 256, 256), 256)
            gate = dot(arr[group(g, last), :], wf[0, :, cols])
            up = dot(arr[group(g, last), :], wf[1, :, cols])
            hid[group(g, last), cols] = (gate / (1.0 + jnp.exp(-gate)) * up).astype(BF16)
            return 0

        lax.fori_loop(0, hid.shape[1] // 256, tile, 0)

    for m in range(3):
        w_local(m).start()
    for j in range(CHUNKS):
        for d in range(2):
            if j == 0:
                go(t_copy(d, 0))
            go(z1_copy(d, 0, j))
    for m in range(3):
        for r in (1, 3):
            go(w_copy(m, r))
        go(f_copy(m, 0))

    route(OWN)
    for k in range(1, HALF + 1):
        for j in range(CHUNKS):
            for d in range(2):
                if j == 0 and (k < HALF or d == 0):
                    t_copy(d, k - 1).wait_recv()
                    if k < HALF - 1 or (k == HALF - 1 and d == 0):
                        go(t_copy(d, k))
                if live(d, k - 1, j):
                    z1_copy(d, k - 1, j).wait_recv()
                if k < HALF and live(d, k, j):
                    go(z1_copy(d, k, j))
        route(k)
        for g, members in enumerate(GROUPS):
            if k == max(members):
                tables(g)
                select(g)
        if k in (2, 3, 5):
            relay_weight({2: 0, 3: 1, 5: 2}[k])
        if k in (5, 6):
            share_weight(k - 5)
    finish_weight(0)
    finish_weight(1)
    hide(0, 2)
    share_weight(2)
    hide(3, 4)
    finish_weight(2)

    def place(i):
        return lax.rem(yi + 1 + i, CHUNKS)

    def back(g, last, i):
        rows = pl.ds(pl.multiple_of(place(i) * cw, cw), cw)
        made = dot(hid[group(g, last), :], wf[2, rows, :], ((1,), (1,))).astype(BF16)
        for n in range(last, g - 1, -1):
            start = STARTS[n] - STARTS[g]
            br[i, block(n, 0)] = made[start : start + ROWS[n]]
            rest = slice(STARTS[n] + ROWS[n], STARTS[n] + X * ROWS[n])
            st2[i, rest] = made[start + ROWS[n] : start + X * ROWS[n]]
            for r in (2, 1, 3):
                go(x2_copy(n, i, r))

    arrived = set()

    def share(k, i):
        total = None
        for g, members in enumerate(GROUPS):
            if k in members:
                if (g, i) not in arrived:
                    arrived.add((g, i))
                    for r in (2, 1, 3):
                        x2_copy(g, i, r).wait_recv()
                part = dot(gt[g][spot(g, k), :], br[i, group(g)])
                total = part if total is None else total + part
        return total

    def reduce_step(i, s):
        part = share(HALF - s, i)
        if s == 0:
            d = 0 if i < CHUNKS // 2 else 1
            rs_s[d, 0, i] = part.astype(BF16)
            go(rs_copy(d, 0, i))
            back(2, 2, i)
        else:
            for d in range(2):
                mine = part[TOK:] if d == 0 else part[:TOK]
                if s > 1 or live(d, HALF - 1, i):
                    rs_copy(d, s - 1, i).wait_recv()
                    mine = mine + rs_r[d, s - 1, i].astype(F32)
                rs_s[d, s, i] = mine.astype(BF16)
                go(rs_copy(d, s, i))
            if s in (1, 2):
                back(2 - s, 2 - s, i)
            if s == 6:
                own[i] = share(OWN, i)

    def finish_tangent(i):
        cols = pl.ds(pl.multiple_of(place(i) * cw, cw), cw)
        total = own[i]
        for d in range(2):
            rs_copy(d, HALF - 1, i).wait_recv()
            total = total + rs_r[d, HALF - 1, i].astype(F32)
        tan_ref[:, cols] = total
        sc[i] = (curv_v[:, cols].astype(F32) * total).astype(BF16)
        for d in range(2):
            go(z3_copy(d, 0, i))

    def scaled_of(k, i):
        if k == OWN:
            return [sc[i]]
        if k == FAR:
            return [zb3[0 if i < CHUNKS // 2 else 1, HALF - 1, i]]
        return [zb3[0, k - 1, i], zb3[1, k - 1, i]]

    def gather_step(i, k):
        for d in range(2):
            if live(d, k - 1, i):
                z3_copy(d, k - 1, i).wait_recv()
            if k < HALF and live(d, k, i):
                go(z3_copy(d, k, i))
        for g, members in enumerate(GROUPS):
            if k == max(members):
                source = jnp.concatenate([t for m in members for t in scaled_of(m, i)], axis=0)
                picked = dot(gm[g][...], source).astype(BF16)
                rr[i, block(g, 0)] = picked[: ROWS[g]]
                st3[i, STARTS[g] + ROWS[g] : STARTS[g] + X * ROWS[g]] = picked[ROWS[g] :]
                for r in (2, 1, 3):
                    go(x3_copy(g, i, r))

    hw = cw // 2

    def pair_copy(i):
        return remote(ps.at[i], pr.at[i], p_s.at[i], p_r.at[i], sibling)

    def home_copy(i):
        return remote(ys.at[i], yr.at[i], y_s.at[i], y_r.at[i], at_y(1 + i))

    def multiply(i):
        for g in range(len(GROUPS)):
            for r in (2, 1, 3):
                x3_copy(g, i, r).wait_recv()
        theirs = pl.ds(pl.multiple_of((1 - ci) * hw, hw), hw)
        mine = pl.ds(pl.multiple_of(ci * hw, hw), hw)
        ps[i] = dot(rr[i, :, theirs], hid[...], ((0,), (0,))).astype(BF16)
        go(pair_copy(i))
        half[i % 2] = dot(rr[i, :, mine], hid[...], ((0,), (0,)))

    def send_home(i):
        pair_copy(i).wait_recv()
        total = half[i % 2] + pr[i].astype(F32)
        if i < Y - 1:
            ys[i] = total.astype(BF16)
            go(home_copy(i))
        else:
            for n in range(Y - 1):
                home_copy(n).wait_recv()
                total = total + yr[n].astype(F32)
            out_ref[...] = total

    for i in range(2):
        back(3, 4, i)
    for tick in range(2 * HALF + 3 + LAG * (CHUNKS - 1)):
        for i in range(CHUNKS):
            u = tick - LAG * i
            if 0 <= u < HALF:
                reduce_step(i, u)
            elif u == HALF:
                finish_tangent(i)
            elif HALF < u <= 2 * HALF:
                gather_step(i, u - HALF)
            elif u == 2 * HALF + 1:
                multiply(i)
            elif u == 2 * HALF + 2:
                send_home(i)
        if tick < CHUNKS - 2:
            back(3, 4, 2 + tick)

    for copy in sends:
        copy.wait_send()


def per_device(activations, curvature, routes, route_gates, w_gate, w_up, v_down):
    tokens, width = activations.shape
    features, hidden = w_gate.shape[1:]
    cw = width // CHUNKS
    table = jnp.concatenate([route_gates.T, routes.T.astype(F32)], axis=1)
    vmem = pl.BlockSpec(memory_space=pltpu.VMEM)
    hbm = pl.BlockSpec(memory_space=pl.ANY)
    dma = pltpu.SemaphoreType.DMA
    n = len(GROUPS)
    scratch = [
        pltpu.VMEM((3, width, hidden), BF16),
        pltpu.VMEM((2, HALF, CHUNKS, tokens, cw), BF16),
        pltpu.VMEM((2, HALF) + table.shape, F32),
        pltpu.VMEM((HALF + 1, 8, PAIR), F32),
        pltpu.VMEM((HALF + 1, 8, PAIR), F32),
    ]
    scratch += [pltpu.VMEM((X * ROWS[g], COLS[g]), BF16) for g in range(n)] * 2
    scratch += [pltpu.VMEM((COLS[g], X * ROWS[g]), BF16) for g in range(n)]
    scratch += [
        pltpu.VMEM((TOTAL, width), BF16),
        pltpu.VMEM((TOTAL, width), BF16),
        pltpu.VMEM((TOTAL, hidden), BF16),
        pltpu.VMEM((CHUNKS, TOTAL, cw), BF16),
        pltpu.VMEM((CHUNKS, TOTAL, cw), BF16),
        pltpu.VMEM((2, HALF, CHUNKS, tokens, cw), BF16),
        pltpu.VMEM((2, HALF, CHUNKS, tokens, cw), BF16),
        pltpu.VMEM((CHUNKS, tokens, cw), BF16),
        pltpu.VMEM((2, HALF, CHUNKS, tokens, cw), BF16),
        pltpu.VMEM((CHUNKS, TOTAL, cw), BF16),
        pltpu.VMEM((CHUNKS, TOTAL, cw), BF16),
        pltpu.VMEM((CHUNKS, tokens, cw), F32),
        pltpu.VMEM((CHUNKS, features, hidden), BF16),
        pltpu.VMEM((CHUNKS, features, hidden), BF16),
        pltpu.VMEM((Y - 1, features, hidden), BF16),
        pltpu.VMEM((Y - 1, features, hidden), BF16),
        pltpu.VMEM((2, features, hidden), F32),
        pltpu.VMEM((tokens, width), BF16),
        pltpu.VMEM((tokens, width), BF16),
        dma((2,)),
        dma((3,)),
        dma((3, 2)), dma((3, 2)),
        dma((3, 2)), dma((3, 2)),
        dma((3, Y)), dma((3, Y)),
        dma((2, HALF, CHUNKS)), dma((2, HALF, CHUNKS)),
        dma((2, HALF)), dma((2, HALF)),
        dma((n, X)), dma((n, X)),
        dma((n, CHUNKS, X)), dma((n, CHUNKS, X)),
        dma((2, HALF, CHUNKS)), dma((2, HALF, CHUNKS)),
        dma((2, HALF, CHUNKS)), dma((2, HALF, CHUNKS)),
        dma((n, CHUNKS, X)), dma((n, CHUNKS, X)),
        dma((CHUNKS,)), dma((CHUNKS,)),
        dma((Y - 1,)), dma((Y - 1,)),
    ]
    tangent, product = pl.pallas_call(
        kernel,
        out_shape=(
            jax.ShapeDtypeStruct((tokens, width), F32),
            jax.ShapeDtypeStruct((features, hidden), F32),
        ),
        in_specs=[hbm, hbm, vmem, hbm, hbm, hbm],
        out_specs=(vmem, vmem),
        scratch_shapes=scratch,
        compiler_params=pltpu.CompilerParams(
            collective_id=0, has_side_effects=True, vmem_limit_bytes=62 * 2**20
        ),
    )(activations, curvature, table, w_gate[0], w_up[0], v_down[0])
    return (tangent, product[None])


def solution(mesh):
    return jax.shard_map(
        per_device,
        mesh=mesh,
        in_specs=(
            P(("dp", "expert"), None),
            P(("dp", "expert"), None),
            P(("dp", "expert"), None),
            P(("dp", "expert"), None),
            P("expert", "dp", None),
            P("expert", "dp", None),
            P("expert", "dp", None),
        ),
        out_specs=(P(("dp", "expert"), None), P("expert", "dp", None)),
        check_vma=False,
    )
```
